256 devices in a mesh: tm: 128 (over z, y, x), seq: 2 (over core).
Axes of the slice: x: 4, y: 4, z: 8, core: 2. Of those that a mesh axis runs over, the one named last changes fastest.
Arguments:
- noise: float32 [8, 128, 64], P(None, 'seq'), may hold values from -6 to 6
- step_size: float32 [128], P('tm'), may hold values from 0.05 to 0.15
- step_ids: int32 [128], P('tm'), may hold values from 0 to 49, as said below
- mod_table: float32 [50, 3, 3072], replicated, may hold values from -3 to 3
- w_in: bfloat16 [64, 3072], replicated
- w_qkv: bfloat16 [3072, 3, 1536], P(None, None, 'seq'), may hold values from -0.109375 to 0.109375
- w_out: bfloat16 [1536, 3072], replicated, may hold values from -1.25 to 1.25
- w_final: bfloat16 [3072, 64], replicated, may hold values from -0.109375 to 0.109375
- text_keys: bfloat16 [256, 1536], P(None, 'seq'), may hold values from -6 to 6
- text_values: bfloat16 [256, 1536], P(None, 'seq'), may hold values from -6 to 6
Outputs:
- trajectory: float32 [128, 128, 64], P('tm', 'seq')
The draws below stay inside these ranges and needn't reach their ends.
Inputs may be any that keep to these rules, and one draw needn't show every extreme that they name: `step_ids`: for each block b, the levels of entries k * 8 + b fall strictly as k rises; the first step of every block is at level 49 and the last at level 0.
All inputs are finite; a program needn't handle non-finite values.
Results may differ from the reference program's by a relative error of at most 0.0035.
Values may be sent and summed in bfloat16 or wider, within the bound.
A program may use at most 128 MiB of HBM per device.

```python
import math
import jax
import jax.numpy as jnp
from jax import lax

D = 3072
HEADS = 12
HD = 128
C = 64
TXT = 256
LEVELS = 50
ITERS = 2
STEPS = 16
TOKENS = 128
GROUPS = 8


def draw_w_in(key, part):
    key = jax.random.fold_in(key, 11)
    entry_key, column_key = jax.random.split(key)
    column_scale = jnp.exp(jax.random.uniform(column_key, (1, D), jnp.float32, math.log(0.3), math.log(3.0)))
    entries = jax.random.normal(entry_key, (C, D), jnp.float32)
    return (entries * column_scale * C ** (-0.5)).astype(jnp.bfloat16)


def falling_levels(block_key):
    inner = jnp.arange(1, LEVELS - 1, dtype=jnp.int32)
    chosen = jax.random.permutation(block_key, inner)[:STEPS - 2]
    middle = -jnp.sort(-chosen)
    top = jnp.full((1,), LEVELS - 1, dtype=jnp.int32)
    bottom = jnp.zeros((1,), dtype=jnp.int32)
    return jnp.concatenate([top, middle.astype(jnp.int32), bottom], axis=0)


def draw_step_ids(key, part):
    key = jax.random.fold_in(key, 5)
    block_keys = jax.random.split(key, GROUPS)
    levels = jax.vmap(falling_levels)(block_keys)
    return jnp.transpose(levels).reshape(STEPS * GROUPS).astype(jnp.int32)


def block_scale(own_key, extent, cuts, low, high):
    factor_of, own = 1.0, jax.random.fold_in(own_key, 6)
    for position, parts in cuts:
        draws = jnp.exp(jax.random.uniform(jax.random.fold_in(own, position), (parts,), jnp.float32, low / len(cuts), high / len(cuts)))
        factor_of = factor_of * jnp.repeat(draws, extent[position] // parts).reshape([-1 if axis == position else 1 for axis in range(len(extent))])
    return factor_of


def bell_draw(own_key, extent, deviation, limit, cuts=(), kind=jnp.bfloat16):
    factor_of = block_scale(own_key, extent, cuts, -0.22, 0.18) if cuts else 1.0
    values = jax.random.normal(own_key, extent, jnp.float32) * deviation * factor_of
    return jnp.minimum(jnp.maximum(values, -limit), limit).astype(kind)


def setup_inputs(seed: int = 0) -> dict:
    keys = jax.random.split(jax.random.key(seed), 11)
    return {
        "noise": bell_draw(keys[0], (GROUPS, TOKENS, C), 1.0, 6.0, ((1, 2),), jnp.float32),
        "step_size": jnp.clip(0.05 + 0.10000001 * jax.random.uniform(keys[1], (GROUPS * STEPS,), jnp.float32) ** block_scale(keys[1], (GROUPS * STEPS,), ((0, 128),), -0.2, 0.2), 0.05, 0.15),
        "step_ids": draw_step_ids(jax.random.fold_in(keys[10], 71), 0),
        "mod_table": bell_draw(keys[3], (LEVELS, 3, D), 0.5, 3.0, (), jnp.float32),
        "w_in": draw_w_in(jax.random.fold_in(keys[10], 71), 0),
        "w_qkv": bell_draw(keys[5], (D, 3, HEADS * HD), D ** -0.5, 0.109375, ((2, 2),)),
        "w_out": bell_draw(keys[6], (HEADS * HD, D), (HEADS * HD // 64) ** -0.5, 1.25),
        "w_final": bell_draw(keys[7], (D, C), D ** -0.5, 0.109375),
        "text_keys": bell_draw(keys[8], (TXT, HEADS * HD), 1.0, 6.0, ((1, 2),)),
        "text_values": bell_draw(keys[9], (TXT, HEADS * HD), 1.0, 6.0, ((1, 2),)),
    }


epsilon = 1e-06

def layer_norm(values):
    average = lax.optimization_barrier(jnp.mean(values, axis=-1, keepdims=True))
    centred = values - average
    spread = lax.optimization_barrier(jnp.mean(centred * centred, axis=-1, keepdims=True))
    return centred * lax.rsqrt(spread + epsilon)

def head_norm(values):
    return values * lax.rsqrt(lax.optimization_barrier(jnp.mean(values * values, axis=-1, keepdims=True)) + epsilon)

def velocity_of(latent, level_index, mod_table, w_in, w_qkv, w_out, w_final, text_normed, text_heads):
    hidden = jnp.dot(latent.astype(jnp.bfloat16), w_in, preferred_element_type=jnp.float32)
    modulation = mod_table[level_index]
    shift_term = modulation[0]
    scale_term = modulation[1]
    gate_term = modulation[2]
    normed = (layer_norm(hidden) * (1.0 + scale_term) + shift_term).astype(jnp.bfloat16)
    projected = jnp.dot(normed, w_qkv.reshape(D, 3 * HEADS * HD), preferred_element_type=jnp.float32)
    projected = projected.reshape(TOKENS, 3, HEADS, HD)
    queries = head_norm(projected[:, 0]).astype(jnp.bfloat16)
    own_keys = head_norm(projected[:, 1]).astype(jnp.bfloat16)
    own_values = projected[:, 2].astype(jnp.bfloat16)
    all_keys = jnp.concatenate([own_keys, text_normed], axis=0)
    all_values = jnp.concatenate([own_values, text_heads], axis=0)
    scores = jnp.einsum('qhd,khd->hqk', queries.astype(jnp.float32), all_keys.astype(jnp.float32)) * HD ** (-0.5)
    exponent = jnp.exp(scores)
    weights = (exponent / lax.optimization_barrier(jnp.sum(exponent, axis=-1, keepdims=True))).astype(jnp.bfloat16)
    attended = jnp.einsum('hqk,khd->qhd', weights.astype(jnp.float32), all_values.astype(jnp.float32))
    attended = attended.astype(jnp.bfloat16).reshape(TOKENS, HEADS * HD)
    projection = jnp.dot(attended, w_out, preferred_element_type=jnp.float32)
    mixed_rows = hidden + gate_term * projection
    final_normed = layer_norm(mixed_rows).astype(jnp.bfloat16)
    return jnp.dot(final_normed, w_final, preferred_element_type=jnp.float32)

def reference(noise, step_size, step_ids, mod_table, w_in, w_qkv, w_out, w_final, text_keys, text_values):
    text_normed = head_norm(text_keys.astype(jnp.float32).reshape(TXT, HEADS, HD)).astype(jnp.bfloat16)
    text_heads = text_values.reshape(TXT, HEADS, HD)

    def drift_of(inputs):
        latent, level_index, step_scale = inputs
        return step_scale * velocity_of(latent, level_index, mod_table, w_in, w_qkv, w_out, w_final, text_normed, text_heads)
    start = jnp.broadcast_to(noise[None], (STEPS, GROUPS, TOKENS, C))
    latent_all = start
    trajectory = start
    for sweep in range(ITERS):
        flat = latent_all.reshape(STEPS * GROUPS, TOKENS, C)
        drifts = lax.map(drift_of, (flat, step_ids, step_size)).reshape(STEPS, GROUPS, TOKENS, C)
        running = jnp.cumsum(drifts, axis=0)
        trajectory = noise[None] + running
        earlier = jnp.concatenate([jnp.zeros((1, GROUPS, TOKENS, C), jnp.float32), running[:-1]], axis=0)
        latent_all = noise[None] + earlier
    return trajectory.reshape(STEPS * GROUPS, TOKENS, C)
```

```python
import functools
import math

import jax
import jax.numpy as jnp
from jax import lax
from jax.experimental import pallas as pl
from jax.experimental.pallas import tpu as pltpu
from jax.sharding import PartitionSpec as P

HD = 128
ITERS = 2
EPS = 1e-06
MESH = pl.DeviceIdType.MESH
F32 = jnp.float32
BF16 = jnp.bfloat16
NT = (((1,), (1,)), ((), ()))


def head_norm(values):
    return values * lax.rsqrt(jnp.mean(values * values, axis=-1, keepdims=True) + EPS)


def kernel(
    groups,
    steps,
    step_size,
    step_ids,
    noise_hbm,
    mod_hbm,
    w_in_hbm,
    w_qkv_hbm,
    w_out_hbm,
    w_fin_hbm,
    tk_hbm,
    tv_hbm,
    out_ref,
    noise_raw,
    noise_p,
    mod_v,
    shift_b,
    scale_b,
    gate_b,
    w_in2,
    w_qkv,
    w_out,
    w_fin,
    w_fin2,
    cs_diff,
    tk,
    tv,
    tk_n,
    lat,
    hidden,
    normed,
    att,
    att_par,
    proj,
    mixed,
    u_mine,
    u_send,
    u_recv,
    d_send,
    d_recv,
    load_sem,
    lat_sem,
    att_sem,
    u_sem,
    d_send_sem,
    d_recv_sem,
):
    tok, chan = noise_raw.shape
    width = hidden.shape[1]
    half = width // 2
    own_cols = w_qkv.shape[2]
    pair_cols = 2 * HD
    pairs = own_cols // pair_cols
    txt = tk.shape[0]
    rows = 2 * tok
    pack = tok // 2

    t = lax.axis_index("tm")
    s = lax.axis_index("seq")
    block = lax.rem(t, groups)
    step = t // groups
    partner = (t, 1 - s)

    counter = iter(range(64))

    def load(src, dst):
        copy = pltpu.make_async_copy(src, dst, load_sem.at[next(counter)])
        copy.start()
        return copy

    half_at = pl.multiple_of(s * half, HD)
    ld_noise = load(noise_hbm.at[block], noise_raw)
    ld_in = [load(w_in_hbm, w_in2.at[pl.ds(i * chan, chan)]) for i in range(2)]
    ld_mod = load(mod_hbm, mod_v)
    ld_tk = load(tk_hbm, tk)
    ld_fin = load(w_fin_hbm, w_fin)
    ld_qkv = []
    for p in range(pairs):
        cols = pl.ds(p * pair_cols, pair_cols)
        ld_qkv.append([load(w_qkv_hbm.at[j, :, cols], w_qkv.at[j, :, cols]) for j in range(3)])
        if p == 0:
            ld_tv = load(tv_hbm, tv)
    ld_out = []
    for i in range(2):
        at = pl.multiple_of((s if i == 0 else 1 - s) * own_cols, HD)
        ld_out.append(load(w_out_hbm.at[pl.ds(at, own_cols), pl.ds(half_at, half)], w_out.at[i]))

    barrier = pltpu.get_barrier_semaphore()
    pl.semaphore_signal(barrier, inc=1, device_id=partner, device_id_type=MESH)

    def greet(j, carry):
        @pl.when(j != step)
        def _():
            pl.semaphore_signal(
                barrier, inc=1, device_id=(j * groups + block, s), device_id_type=MESH
            )

        return carry

    lax.fori_loop(0, steps, greet, 0)
    pl.semaphore_wait(barrier, steps)

    lane = lax.broadcasted_iota(jnp.int32, (pack, 2 * chan), 1)
    low = lane < chan

    def put_latent(packed):
        lat[0:pack, :] = jnp.where(low, packed, 0.0).astype(BF16)
        lat[pack:tok, :] = jnp.where(low, 0.0, packed).astype(BF16)

    ld_noise.wait()
    raw = noise_raw[...]
    noise_p[...] = jnp.concatenate([raw[0:pack], raw[pack:tok]], axis=1)
    put_latent(noise_p[...])

    def lat_copy():
        return pltpu.make_async_remote_copy(
            src_ref=lat.at[pl.ds(0, tok)],
            dst_ref=lat.at[pl.ds(tok, tok)],
            send_sem=lat_sem.at[0],
            recv_sem=lat_sem.at[1],
            device_id=partner,
            device_id_type=MESH,
        )

    offsets = sorted(range(1, steps), key=lambda o: abs(o - steps // 2))
    size = step_size[0]

    for sweep in range(ITERS):
        moving = lat_copy()
        moving.start()
        if sweep == 0:
            for c in ld_in:
                c.wait()
        for part in range(2):
            at = pl.ds(part * tok, tok)
            if part == 1:
                moving.wait()
            for c0 in range(0, width, 512):
                cs = pl.ds(c0, 512)
                hidden[at, cs] = jnp.dot(lat[at, :], w_in2[:, cs], preferred_element_type=F32)
            if sweep == 0 and part == 0:
                ld_mod.wait()
                level = step_ids[0]
                ones = jnp.ones((8, 1), F32)
                shift_b[...] = ones * mod_v[0, pl.ds(level, 1), :]
                scale_b[...] = ones * (1.0 + mod_v[1, pl.ds(level, 1), :])
                gate_b[...] = ones * mod_v[2, pl.ds(level, 1), :]
            for r0 in range(part * tok, part * tok + tok, 16):
                rs = pl.ds(r0, 16)
                h = hidden[rs, :]
                mean = jnp.sum(h, axis=-1, keepdims=True) * (1.0 / width)
                c = h - mean
                var = jnp.sum(c * c, axis=-1, keepdims=True) * (1.0 / width)
                n = (c * lax.rsqrt(var + EPS)).reshape(2, 8, width)
                n = n * scale_b[...][None] + shift_b[...][None]
                normed[rs, :] = n.reshape(16, width).astype(BF16)
        if sweep == 0:
            ld_tk.wait()
            for h0 in range(0, own_cols, HD):
                hs = pl.ds(h0, HD)
                tk_n[:, hs] = head_norm(tk[:, hs].astype(F32)).astype(BF16)
            ld_fin.wait()
            fin = w_fin[...]
            w_fin2[0:chan, :] = w_fin[:, pl.ds(half_at, half)]
            w_fin2[chan : 2 * chan, :] = w_fin[:, pl.ds(half_at, half)]
            one = jnp.ones((8, half), BF16)
            cs_own = lax.dot_general(one, w_fin2[...], NT, preferred_element_type=F32)
            cs_all = lax.dot_general(
                jnp.ones((8, width), BF16),
                jnp.concatenate([fin, fin], axis=0),
                NT,
                preferred_element_type=F32,
            )
            cs_diff[...] = 2.0 * cs_own - cs_all

        att_moves = []
        for p in range(pairs):
            cols = pl.ds(p * pair_cols, pair_cols)
            if sweep == 0:
                for c in ld_qkv[p]:
                    c.wait()
                if p == 0:
                    ld_tv.wait()
            q2, k2, v2 = [
                jnp.dot(normed[...], w_qkv[j, :, cols], preferred_element_type=F32)
                for j in range(3)
            ]
            for i in range(2):
                hs = slice(i * HD, (i + 1) * HD)
                at = pl.ds(p * pair_cols + i * HD, HD)
                q = head_norm(q2[:, hs]).astype(BF16)
                k = head_norm(k2[:, hs]).astype(BF16)
                v = v2[:, hs].astype(BF16)
                factor = HD ** (-0.5) * math.log2(math.e)
                own = lax.dot_general(q, k, NT, preferred_element_type=F32)
                far = lax.dot_general(q, tk_n[:, at], NT, preferred_element_type=F32)
                own = jnp.exp2(own * factor)
                far = jnp.exp2(far * factor)
                total = jnp.sum(own, axis=-1, keepdims=True) + jnp.sum(
                    far, axis=-1, keepdims=True
                )
                mix = jnp.dot(own.astype(BF16), v, preferred_element_type=F32)
                mix = mix + jnp.dot(far.astype(BF16), tv[:, at], preferred_element_type=F32)
                att[:, at] = (mix / total).astype(BF16)
            for i in range(2):
                c = pltpu.make_async_remote_copy(
                    src_ref=att.at[pl.ds(i * tok, tok), cols],
                    dst_ref=att_par.at[pl.ds((1 - i) * tok, tok), cols],
                    send_sem=att_sem.at[0, p, i],
                    recv_sem=att_sem.at[1, p, i],
                    device_id=partner,
                    device_id_type=MESH,
                )
                c.start()
                att_moves.append(c)

        if sweep == 0:
            ld_out[0].wait()
        for c0 in range(0, half, 512):
            cs = pl.ds(c0, 512)
            proj[:, cs] = jnp.dot(att[...], w_out[0, :, cs], preferred_element_type=F32)
        if sweep == 0:
            ld_out[1].wait()
        for c in att_moves:
            c.wait()
        for c0 in range(0, half, 512):
            cs = pl.ds(c0, 512)
            from_par = jnp.dot(att_par[...], w_out[1, :, cs], preferred_element_type=F32)
            there = pl.ds(pl.multiple_of(half_at + c0, HD), 512)
            gate = gate_b[0:1, there]
            mixed[:, cs] = hidden[:, there] + gate * (proj[:, cs] + from_par)

        for r0 in range(0, rows, 16):
            rs = pl.ds(r0, 16)
            m = mixed[rs, :]
            mean = jnp.sum(m, axis=-1, keepdims=True) * (1.0 / half)
            c = m - mean
            square = jnp.sum(c * c, axis=-1, keepdims=True)
            u = lax.dot_general(c.astype(BF16), w_fin2[...], NT, preferred_element_type=F32)
            dst = u_mine if r0 < tok else u_send
            ds = pl.ds(r0 % tok, 16)
            dst[0, ds, :] = u
            dst[1, ds, :] = jnp.broadcast_to(mean, (16, 2 * chan))
            dst[2, ds, :] = jnp.broadcast_to(square, (16, 2 * chan))
        c = pltpu.make_async_remote_copy(
            src_ref=u_send,
            dst_ref=u_recv,
            send_sem=u_sem.at[0],
            recv_sem=u_sem.at[1],
            device_id=partner,
            device_id_type=MESH,
        )
        c.start()
        c.wait()
        delta = (u_mine[1] - u_recv[1]) * 0.5
        var = (u_mine[2] + u_recv[2]) * (1.0 / width) + delta * delta
        velocity = u_mine[0] + u_recv[0] + delta * cs_diff[0:1, :]
        velocity = velocity * lax.rsqrt(var + EPS) * size
        drift = jnp.where(low, velocity[0:pack], velocity[pack:tok])
        d_send[sweep] = drift.astype(BF16)

        def send_to(j):
            return pltpu.make_async_remote_copy(
                src_ref=d_send.at[sweep],
                dst_ref=d_recv.at[sweep, step],
                send_sem=d_send_sem.at[sweep],
                recv_sem=d_recv_sem.at[sweep, step],
                device_id=(j * groups + block, s),
                device_id_type=MESH,
            )

        for o in offsets:

            @pl.when(step + o < steps)
            def _():
                send_to(step + o).start()

        def take(j, total):
            pltpu.make_async_remote_copy(
                src_ref=d_send.at[sweep],
                dst_ref=d_recv.at[sweep, j],
                send_sem=d_send_sem.at[sweep],
                recv_sem=d_recv_sem.at[sweep, j],
                device_id=partner,
                device_id_type=MESH,
            ).wait_recv()
            return total + d_recv[sweep, j].astype(F32)

        earlier = lax.fori_loop(0, step, take, jnp.zeros((pack, 2 * chan), F32))
        if sweep < ITERS - 1:
            put_latent(noise_p[...] + earlier)
        else:
            final = noise_p[...] + (earlier + drift)
            out_ref[0:pack, :] = final[:, 0:chan]
            out_ref[pack:tok, :] = final[:, chan : 2 * chan]

        def sent(j, carry):
            send_to(j).wait_send()
            return carry

        lax.fori_loop(step + 1, steps, sent, 0)


def per_device(
    noise, step_size, step_ids, mod_table, w_in, w_qkv, w_out, w_final, text_keys, text_values
):
    groups, tok, chan = noise.shape
    steps = lax.axis_size("tm") // groups
    width = w_in.shape[1]
    half = width // 2
    txt, own_cols = text_keys.shape
    levels = mod_table.shape[0]
    pairs = own_cols // (2 * HD)
    rows = 2 * tok
    pack = tok // 2
    any_spec = pl.BlockSpec(memory_space=pl.ANY)
    smem = pl.BlockSpec(memory_space=pltpu.SMEM)
    vm = pltpu.VMEM
    dma = pltpu.SemaphoreType.DMA
    out = pl.pallas_call(
        functools.partial(kernel, groups, steps),
        out_shape=jax.ShapeDtypeStruct((tok, chan), F32),
        in_specs=[smem, smem] + [any_spec] * 8,
        out_specs=pl.BlockSpec(memory_space=pltpu.VMEM),
        scratch_shapes=[
            vm((tok, chan), F32),
            vm((pack, 2 * chan), F32),
            vm((3, levels, width), F32),
            vm((8, width), F32),
            vm((8, width), F32),
            vm((8, width), F32),
            vm((2 * chan, width), BF16),
            vm((3, width, own_cols), BF16),
            vm((2, own_cols, half), BF16),
            vm((chan, width), BF16),
            vm((2 * chan, half), BF16),
            vm((8, 2 * chan), F32),
            vm((txt, own_cols), BF16),
            vm((txt, own_cols), BF16),
            vm((txt, own_cols), BF16),
            vm((rows, 2 * chan), BF16),
            vm((rows, width), F32),
            vm((rows, width), BF16),
            vm((rows, own_cols), BF16),
            vm((rows, own_cols), BF16),
            vm((rows, half), F32),
            vm((rows, half), F32),
            vm((3, tok, 2 * chan), F32),
            vm((3, tok, 2 * chan), F32),
            vm((3, tok, 2 * chan), F32),
            vm((ITERS, pack, 2 * chan), BF16),
            vm((ITERS, steps, pack, 2 * chan), BF16),
            dma((24,)),
            dma((2,)),
            dma((2, pairs, 2)),
            dma((2,)),
            dma((ITERS,)),
            dma((ITERS, steps)),
        ],
        compiler_params=pltpu.CompilerParams(
            collective_id=0, has_side_effects=True, vmem_limit_bytes=56 * 2**20
        ),
        cost_estimate=pl.CostEstimate(
            flops=5 * 10**9, bytes_accessed=25 * 10**6, transcendentals=10**6
        ),
        name="picard",
    )(
        step_size,
        step_ids,
        noise,
        jnp.transpose(mod_table, (1, 0, 2)),
        w_in,
        jnp.transpose(w_qkv, (1, 0, 2)),
        w_out,
        jnp.transpose(w_final, (1, 0)),
        text_keys,
        text_values,
    )
    return out[None]


def solution(mesh):
    placed = (
        P(None, "seq", None),
        P("tm"),
        P("tm"),
        P(),
        P(),
        P(None, None, "seq"),
        P(),
        P(),
        P(None, "seq"),
        P(None, "seq"),
    )
    return jax.shard_map(
        per_device, mesh=mesh, in_specs=placed, out_specs=P("tm", "seq", None), check_vma=False
    )
```

```python
import functools
import math

import jax
import jax.numpy as jnp
from jax import lax
from jax.experimental import pallas as pl
from jax.experimental.pallas import tpu as pltpu
from jax.sharding import PartitionSpec as P

HD = 128
ITERS = 2
EPS = 1e-06
MESH = pl.DeviceIdType.MESH
F32 = jnp.float32
BF16 = jnp.bfloat16
NT = (((1,), (1,)), ((), ()))


def head_norm(values):
    return values * lax.rsqrt(jnp.mean(values * values, axis=-1, keepdims=True) + EPS)


def kernel(
    groups,
    steps,
    step_size_hbm,
    step_ids_hbm,
    noise_hbm,
    mod_hbm,
    w_in_hbm,
    w_qkv_hbm,
    w_out_hbm,
    w_fin_hbm,
    tk_hbm,
    tv_hbm,
    out_ref,
    size_s,
    level_s,
    noise_raw,
    noise_p,
    mod_v,
    gate_v,
    shift_b,
    scale_b,
    gate_b,
    w_in2,
    w_qkv,
    w_out,
    w_fin,
    w_fin_t,
    cs_diff,
    tk,
    tv,
    tk_t,
    lat,
    hidden,
    normed,
    q_s,
    k_s,
    v_s,
    q_n,
    k_n,
    p_s,
    l_s,
    att,
    att_par,
    proj,
    mixed,
    centred,
    u_mine,
    u_send,
    u_recv,
    d_send,
    d_recv,
    load_sem,
    lat_sem,
    att_sem,
    u_sem,
    d_send_sem,
    d_recv_sem,
):
    tok, chan = noise_raw.shape
    width = hidden.shape[1]
    half = width // 2
    own_cols = w_qkv.shape[2]
    heads = own_cols // HD
    pair_cols = 2 * HD
    pairs = own_cols // pair_cols
    txt = tk.shape[0]
    rows = 2 * tok
    keys = rows + txt
    pack = tok // 2

    t = lax.axis_index("tm")
    s = lax.axis_index("seq")
    block = lax.rem(t, groups)
    step = t // groups
    partner = (t, 1 - s)

    counter = iter(range(64))

    def load(src, dst):
        copy = pltpu.make_async_copy(src, dst, load_sem.at[next(counter)])
        copy.start()
        return copy

    half_at = pl.multiple_of(s * half, HD)
    ld_noise = load(noise_hbm.at[block], noise_raw)
    ld_ids = load(step_ids_hbm, level_s)
    ld_size = load(step_size_hbm, size_s)
    ld_in = load(w_in_hbm, w_in2.at[pl.ds(0, chan)])
    ld_mod = load(mod_hbm.at[pl.ds(0, 2)], mod_v)
    ld_tk = load(tk_hbm, tk)
    ld_qkv = []
    for j in range(3):
        if j == 2:
            ld_tv = load(tv_hbm, tv)
            ld_fin = load(w_fin_hbm, w_fin)
        for p in range(pairs):
            cols = pl.ds(p * pair_cols, pair_cols)
            ld_qkv.append(load(w_qkv_hbm.at[j, :, cols], w_qkv.at[j, :, cols]))
    ld_out = []
    for i in range(2):
        at = pl.multiple_of((s if i == 0 else 1 - s) * own_cols, HD)
        ld_out.append(load(w_out_hbm.at[pl.ds(at, own_cols), pl.ds(half_at, half)], w_out.at[i]))
        if i == 0:
            ld_gate = load(mod_hbm.at[2], gate_v)

    barrier = pltpu.get_barrier_semaphore()

    @pl.when(s == 0)
    def _():
        pl.semaphore_signal(barrier, inc=1, device_id=partner, device_id_type=MESH)

    lane = lax.broadcasted_iota(jnp.int32, (pack, 2 * chan), 1)
    low = lane < chan

    def put_latent(packed):
        lat[0:pack, :] = jnp.where(low, packed, 0.0).astype(BF16)
        lat[pack:tok, :] = jnp.where(low, 0.0, packed).astype(BF16)

    ld_noise.wait()
    raw = noise_raw[...]
    noise_p[...] = jnp.concatenate([raw[0:pack], raw[pack:tok]], axis=1)
    put_latent(noise_p[...])

    lat_move = pltpu.make_async_remote_copy(
        src_ref=lat.at[pl.ds(0, tok)],
        dst_ref=lat.at[pl.ds(tok, tok)],
        send_sem=lat_sem.at[0],
        recv_sem=lat_sem.at[1],
        device_id=partner,
        device_id_type=MESH,
    )

    def att_move(p, i):
        cols = pl.ds(p * pair_cols, pair_cols)
        return pltpu.make_async_remote_copy(
            src_ref=att.at[pl.ds(i * tok, tok), cols],
            dst_ref=att_par.at[pl.ds((1 - i) * tok, tok), cols],
            send_sem=att_sem.at[0, p, i],
            recv_sem=att_sem.at[1, p, i],
            device_id=partner,
            device_id_type=MESH,
        )

    u_move = pltpu.make_async_remote_copy(
        src_ref=u_send,
        dst_ref=u_recv,
        send_sem=u_sem.at[0],
        recv_sem=u_sem.at[1],
        device_id=partner,
        device_id_type=MESH,
    )

    def embed(part):
        at = pl.ds(part * tok, tok)
        for c0 in range(0, width, 512):
            cs = pl.ds(c0, 512)
            hidden[at, cs] = jnp.dot(lat[at, :], w_in2[:, cs], preferred_element_type=F32)

    def modulate(part):
        for r0 in range(part * tok, part * tok + tok, 16):
            rs = pl.ds(r0, 16)
            total = jnp.zeros((16, HD), F32)
            for c0 in range(0, width, HD):
                total = total + hidden[rs, pl.ds(c0, HD)]
            mean = jnp.sum(total, axis=-1, keepdims=True) * (1.0 / width)
            mean = jnp.broadcast_to(mean, (16, HD))
            total = jnp.zeros((16, HD), F32)
            for c0 in range(0, width, HD):
                c = hidden[rs, pl.ds(c0, HD)] - mean
                total = total + c * c
            var = jnp.sum(total, axis=-1, keepdims=True) * (1.0 / width)
            rstd = jnp.broadcast_to(lax.rsqrt(var + EPS), (16, HD))
            for c0 in range(0, width, HD):
                cs = pl.ds(c0, HD)
                n = (hidden[rs, cs] - mean) * rstd
                scale = jnp.concatenate([scale_b[:, cs]] * 2, axis=0)
                shift = jnp.concatenate([shift_b[:, cs]] * 2, axis=0)
                normed[rs, cs] = (n * scale + shift).astype(BF16)

    def project(j, p):
        cols = pl.ds(p * pair_cols, pair_cols)
        dst = (q_s, k_s, v_s)[j]
        dst[:, cols] = jnp.dot(
            normed[...], w_qkv[j, :, cols], preferred_element_type=F32
        ).astype(dst.dtype)

    def norm_heads(src, dst):
        for h in range(heads):
            at = pl.ds(h * HD, HD)
            dst[:, at] = head_norm(src[:, at]).astype(BF16)

    factor = HD ** (-0.5) * math.log2(math.e)

    def score(h):
        at = pl.ds(h * HD, HD)
        q = q_n[:, at]
        own = lax.dot_general(q, k_n[:, at], NT, preferred_element_type=F32)
        far = jnp.dot(q, tk_t[at, :], preferred_element_type=F32)
        own = jnp.exp2(own * factor)
        far = jnp.exp2(far * factor)
        p_s[h, :, 0:rows] = own.astype(BF16)
        p_s[h, :, rows:keys] = far.astype(BF16)
        total = jnp.sum(own, axis=-1, keepdims=True) + jnp.sum(far, axis=-1, keepdims=True)
        l_s[h] = jnp.broadcast_to(total, (rows, HD))

    def weigh(h):
        at = pl.ds(h * HD, HD)
        mix = jnp.dot(p_s[h, :, 0:rows], v_s[:, at], preferred_element_type=F32)
        mix = mix + jnp.dot(p_s[h, :, rows:keys], tv[:, at], preferred_element_type=F32)
        att[:, at] = (mix / l_s[h]).astype(BF16)

    offsets = sorted(range(1, steps), key=lambda o: abs(o - steps // 2))

    for sweep in range(ITERS):
        first = sweep == 0
        if first:

            @pl.when(s == 1)
            def _():
                pl.semaphore_wait(barrier, 1)
                lat_move.start()

            ld_in.wait()
            w_in2[chan : 2 * chan, :] = w_in2[0:chan, :]
        else:
            lat_move.start()
        embed(0)
        if first:
            ld_ids.wait()
            ld_mod.wait()
            level = level_s[0]
            ones = jnp.ones((8, 1), F32)
            shift_b[...] = ones * mod_v[0, pl.ds(level, 1), :]
            scale_b[...] = ones * (1.0 + mod_v[1, pl.ds(level, 1), :])
        modulate(0)
        lat_move.wait_recv()
        if first:

            @pl.when(s == 0)
            def _():
                lat_move.start()

                def greet(j, carry):
                    @pl.when(j != step)
                    def _():
                        pl.semaphore_signal(
                            barrier, inc=1, device_id=(j * groups + block, 0), device_id_type=MESH
                        )

                    return carry

                lax.fori_loop(0, steps, greet, 0)

        embed(1)
        modulate(1)
        lat_move.wait_send()
        if first:
            ld_tk.wait()
            for h0 in range(0, own_cols, HD):
                hs = pl.ds(h0, HD)
                tk_t[hs, :] = jnp.transpose(head_norm(tk[:, hs].astype(F32))).astype(BF16)

        for j in range(3):
            if first and j == 2:
                ld_tv.wait()
                ld_fin.wait()
                one = jnp.ones((8, width), BF16)
                both = jnp.concatenate([w_fin[...]] * 2, axis=0)
                cs_all = lax.dot_general(one, both, NT, preferred_element_type=F32)
                for c0 in range(0, half, HD):
                    piece = w_fin[:, pl.ds(pl.multiple_of(half_at + c0, HD), HD)].astype(F32)
                    piece = jnp.concatenate([piece, piece], axis=0)
                    w_fin_t[pl.ds(c0, HD), :] = jnp.transpose(piece).astype(BF16)
                cs_own = jnp.dot(one[:, 0:half], w_fin_t[...], preferred_element_type=F32)
                cs_diff[...] = 2.0 * cs_own - cs_all
            for p in range(pairs):
                if first:
                    ld_qkv[j * pairs + p].wait()
                project(j, p)
                if j == 2:
                    for h in (2 * p, 2 * p + 1):
                        weigh(h)
                    for i in range(2):
                        att_move(p, i).start()
            if j == 0:
                norm_heads(q_s, q_n)
            if j == 1:
                norm_heads(k_s, k_n)
                for h in range(heads):
                    score(h)

        if first:
            ld_out[0].wait()
        for c0 in range(0, half, 512):
            cs = pl.ds(c0, 512)
            proj[:, cs] = jnp.dot(att[...], w_out[0, :, cs], preferred_element_type=F32)
        if first:
            ld_out[1].wait()
            ld_gate.wait()
            gate_b[...] = ones * gate_v[pl.ds(level, 1), :]
        for p in range(pairs):
            for i in range(2):
                att_move(p, i).wait()
        for c0 in range(0, half, 512):
            cs = pl.ds(c0, 512)
            from_par = jnp.dot(att_par[...], w_out[1, :, cs], preferred_element_type=F32)
            there = pl.ds(pl.multiple_of(half_at + c0, HD), 512)
            gate = gate_b[0:1, there]
            mixed[:, cs] = hidden[:, there] + gate * (proj[:, cs] + from_par)

        for r0 in range(0, rows, 16):
            rs = pl.ds(r0, 16)
            m = mixed[rs, :]
            mean = jnp.sum(m, axis=-1, keepdims=True) * (1.0 / half)
            c = m - mean
            square = jnp.sum(c * c, axis=-1, keepdims=True)
            centred[rs, :] = c.astype(BF16)
            dst = u_mine if r0 < tok else u_send
            ds = pl.ds(r0 % tok, 16)
            dst[1, ds, :] = jnp.broadcast_to(mean, (16, 2 * chan))
            dst[2, ds, :] = jnp.broadcast_to(square, (16, 2 * chan))
        u = jnp.dot(centred[...], w_fin_t[...], preferred_element_type=F32)
        u_mine[0] = u[0:tok]
        u_send[0] = u[tok:rows]
        if first:

            @pl.when(s == 0)
            def _():
                pl.semaphore_wait(barrier, steps - 1)

            ld_size.wait()
        u_move.start()
        u_move.wait()
        delta = (u_mine[1] - u_recv[1]) * 0.5
        var = (u_mine[2] + u_recv[2]) * (1.0 / width) + delta * delta
        velocity = u_mine[0] + u_recv[0] + delta * cs_diff[0:1, :]
        velocity = velocity * lax.rsqrt(var + EPS) * size_s[0]
        drift = jnp.where(low, velocity[0:pack], velocity[pack:tok])
        d_send[sweep] = drift.astype(BF16)

        def send_to(j):
            return pltpu.make_async_remote_copy(
                src_ref=d_send.at[sweep],
                dst_ref=d_recv.at[sweep, step],
                send_sem=d_send_sem.at[sweep],
                recv_sem=d_recv_sem.at[sweep, step],
                device_id=(j * groups + block, s),
                device_id_type=MESH,
            )

        for o in offsets:

            @pl.when(step + o < steps)
            def _():
                send_to(step + o).start()

        def take(j, total):
            pltpu.make_async_remote_copy(
                src_ref=d_send.at[sweep],
                dst_ref=d_recv.at[sweep, j],
                send_sem=d_send_sem.at[sweep],
                recv_sem=d_recv_sem.at[sweep, j],
                device_id=partner,
                device_id_type=MESH,
            ).wait_recv()
            return total + d_recv[sweep, j].astype(F32)

        earlier = lax.fori_loop(0, step, take, jnp.zeros((pack, 2 * chan), F32))
        if sweep < ITERS - 1:
            put_latent(noise_p[...] + earlier)
        else:
            final = noise_p[...] + (earlier + drift)
            out_ref[0:pack, :] = final[:, 0:chan]
            out_ref[pack:tok, :] = final[:, chan : 2 * chan]

        def sent(j, carry):
            send_to(j).wait_send()
            return carry

        lax.fori_loop(step + 1, steps, sent, 0)


def per_device(
    noise, step_size, step_ids, mod_table, w_in, w_qkv, w_out, w_final, text_keys, text_values
):
    groups, tok, chan = noise.shape
    steps = lax.axis_size("tm") // groups
    width = w_in.shape[1]
    half = width // 2
    txt, own_cols = text_keys.shape
    levels = mod_table.shape[0]
    heads = own_cols // HD
    pairs = heads // 2
    rows = 2 * tok
    pack = tok // 2
    any_spec = pl.BlockSpec(memory_space=pl.ANY)
    vm = pltpu.VMEM
    dma = pltpu.SemaphoreType.DMA
    out = pl.pallas_call(
        functools.partial(kernel, groups, steps),
        out_shape=jax.ShapeDtypeStruct((tok, chan), F32),
        in_specs=[any_spec] * 10,
        out_specs=pl.BlockSpec(memory_space=pltpu.VMEM),
        scratch_shapes=[
            pltpu.SMEM((1,), F32),
            pltpu.SMEM((1,), jnp.int32),
            vm((tok, chan), F32),
            vm((pack, 2 * chan), F32),
            vm((2, levels, width), F32),
            vm((levels, width), F32),
            vm((8, width), F32),
            vm((8, width), F32),
            vm((8, width), F32),
            vm((2 * chan, width), BF16),
            vm((3, width, own_cols), BF16),
            vm((2, own_cols, half), BF16),
            vm((chan, width), BF16),
            vm((half, 2 * chan), BF16),
            vm((8, 2 * chan), F32),
            vm((txt, own_cols), BF16),
            vm((txt, own_cols), BF16),
            vm((own_cols, txt), BF16),
            vm((rows, 2 * chan), BF16),
            vm((rows, width), F32),
            vm((rows, width), BF16),
            vm((rows, own_cols), F32),
            vm((rows, own_cols), F32),
            vm((rows, own_cols), BF16),
            vm((rows, own_cols), BF16),
            vm((rows, own_cols), BF16),
            vm((heads, rows, rows + txt), BF16),
            vm((heads, rows, HD), F32),
            vm((rows, own_cols), BF16),
            vm((rows, own_cols), BF16),
            vm((rows, half), F32),
            vm((rows, half), F32),
            vm((rows, half), BF16),
            vm((3, tok, 2 * chan), F32),
            vm((3, tok, 2 * chan), F32),
            vm((3, tok, 2 * chan), F32),
            vm((ITERS, pack, 2 * chan), BF16),
            vm((ITERS, steps, pack, 2 * chan), BF16),
            dma((24,)),
            dma((2,)),
            dma((2, pairs, 2)),
            dma((2,)),
            dma((ITERS,)),
            dma((ITERS, steps)),
        ],
        compiler_params=pltpu.CompilerParams(
            collective_id=0, has_side_effects=True, vmem_limit_bytes=56 * 2**20
        ),
        cost_estimate=pl.CostEstimate(
            flops=5 * 10**9, bytes_accessed=25 * 10**6, transcendentals=10**6
        ),
        name="picard",
    )(
        step_size,
        step_ids,
        noise,
        jnp.transpose(mod_table, (1, 0, 2)),
        w_in,
        jnp.transpose(w_qkv, (1, 0, 2)),
        w_out,
        jnp.transpose(w_final, (1, 0)),
        text_keys,
        text_values,
    )
    return out[None]


def solution(mesh):
    placed = (
        P(None, "seq", None),
        P("tm"),
        P("tm"),
        P(),
        P(),
        P(None, None, "seq"),
        P(),
        P(),
        P(None, "seq"),
        P(None, "seq"),
    )
    return jax.shard_map(
        per_device, mesh=mesh, in_specs=placed, out_specs=P("tm", "seq", None), check_vma=False
    )
```

```python
import functools
import math

import jax
import jax.numpy as jnp
from jax import lax
from jax.experimental import pallas as pl
from jax.experimental.pallas import tpu as pltpu
from jax.sharding import PartitionSpec as P

HD = 128
ITERS = 2
EPS = 1e-06
MESH = pl.DeviceIdType.MESH
F32 = jnp.float32
BF16 = jnp.bfloat16
NT = (((1,), (1,)), ((), ()))


def head_norm(values):
    return values * lax.rsqrt(jnp.mean(values * values, axis=-1, keepdims=True) + EPS)


def kernel(
    groups,
    steps,
    step_size_hbm,
    step_ids_hbm,
    noise_hbm,
    mod_hbm,
    w_in_hbm,
    w_qkv_hbm,
    w_out_hbm,
    w_fin_hbm,
    tk_hbm,
    tv_hbm,
    out_ref,
    size_s,
    level_s,
    noise_raw,
    noise_p,
    mod_v,
    gate_v,
    shift_b,
    scale_b,
    gate_b,
    w_in2,
    w_qkv,
    w_out,
    w_fin,
    w_fin_t,
    cs_diff,
    tk,
    tv,
    tk_t,
    lat,
    hidden,
    normed,
    q_s,
    k_s,
    v_s,
    q_n,
    k_n,
    p_s,
    l_s,
    att,
    att_par,
    proj,
    mixed,
    centred,
    u_mine,
    u_send,
    u_recv,
    d_send,
    d_recv,
    load_sem,
    in_sem,
    lat_sem,
    att_sem,
    u_sem,
    d_send_sem,
    d_recv_sem,
):
    tok, chan = noise_raw.shape
    width = hidden.shape[1]
    half = width // 2
    own_cols = w_qkv.shape[2]
    heads = own_cols // HD
    pair_cols = 2 * HD
    pairs = own_cols // pair_cols
    txt = tk.shape[0]
    rows = 2 * tok
    keys = rows + txt
    pack = tok // 2

    t = lax.axis_index("tm")
    s = lax.axis_index("seq")
    block = lax.rem(t, groups)
    step = t // groups
    partner = (t, 1 - s)

    barrier = pltpu.get_barrier_semaphore()

    @pl.when(s == 0)
    def _():
        pl.semaphore_signal(barrier, inc=1, device_id=partner, device_id_type=MESH)

    counter = iter(range(64))

    def load(src, dst):
        copy = pltpu.make_async_copy(src, dst, load_sem.at[next(counter)])
        copy.start()
        return copy

    half_at = pl.multiple_of(s * half, HD)
    ld_noise = load(noise_hbm.at[block], noise_raw)
    ld_ids = load(step_ids_hbm, level_s)
    ld_size = load(step_size_hbm, size_s)
    ld_in = load(w_in_hbm, w_in2.at[pl.ds(0, chan)])
    ld_mod = load(mod_hbm.at[pl.ds(0, 2)], mod_v)
    ld_tk = load(tk_hbm, tk)
    ld_qkv = []
    for j in range(3):
        if j == 1:
            ld_fin = load(w_fin_hbm, w_fin)
        if j == 2:
            ld_tv = load(tv_hbm, tv)
        for p in range(pairs):
            cols = pl.ds(p * pair_cols, pair_cols)
            ld_qkv.append(load(w_qkv_hbm.at[j, :, cols], w_qkv.at[j, :, cols]))
    ld_out = []
    for i in range(2):
        at = pl.multiple_of((s if i == 0 else 1 - s) * own_cols, HD)
        ld_out.append(load(w_out_hbm.at[pl.ds(at, own_cols), pl.ds(half_at, half)], w_out.at[i]))
        if i == 0:
            ld_gate = load(mod_hbm.at[2], gate_v)

    @pl.when(s == 1)
    def _():
        pl.semaphore_wait(barrier, 1)
        pl.semaphore_signal(in_sem, inc=1, device_id=partner, device_id_type=MESH)

    @pl.when(s == 0)
    def _():
        pl.semaphore_wait(in_sem, 1)

        def greet(j, carry):
            @pl.when(j != step)
            def _():
                pl.semaphore_signal(
                    barrier, inc=1, device_id=(j * groups + block, 0), device_id_type=MESH
                )

            return carry

        lax.fori_loop(0, steps, greet, 0)

    lane = lax.broadcasted_iota(jnp.int32, (pack, 2 * chan), 1)
    low = lane < chan

    def put_latent(packed):
        lat[0:pack, :] = jnp.where(low, packed, 0.0).astype(BF16)
        lat[pack:tok, :] = jnp.where(low, 0.0, packed).astype(BF16)

    ld_noise.wait()
    raw = noise_raw[...]
    noise_p[...] = jnp.concatenate([raw[0:pack], raw[pack:tok]], axis=1)
    put_latent(noise_p[...])

    lat_move = pltpu.make_async_remote_copy(
        src_ref=lat.at[pl.ds(0, tok)],
        dst_ref=lat.at[pl.ds(tok, tok)],
        send_sem=lat_sem.at[0],
        recv_sem=lat_sem.at[1],
        device_id=partner,
        device_id_type=MESH,
    )

    def att_move(p, i):
        cols = pl.ds(p * pair_cols, pair_cols)
        return pltpu.make_async_remote_copy(
            src_ref=att.at[pl.ds(i * tok, tok), cols],
            dst_ref=att_par.at[pl.ds((1 - i) * tok, tok), cols],
            send_sem=att_sem.at[0, p, i],
            recv_sem=att_sem.at[1, p, i],
            device_id=partner,
            device_id_type=MESH,
        )

    u_move = pltpu.make_async_remote_copy(
        src_ref=u_send,
        dst_ref=u_recv,
        send_sem=u_sem.at[0],
        recv_sem=u_sem.at[1],
        device_id=partner,
        device_id_type=MESH,
    )

    def embed(part):
        at = pl.ds(part * tok, tok)
        for c0 in range(0, width, 512):
            cs = pl.ds(c0, 512)
            hidden[at, cs] = jnp.dot(lat[at, :], w_in2[:, cs], preferred_element_type=F32)

    def modulate(part):
        for r0 in range(part * tok, part * tok + tok, 16):
            rs = pl.ds(r0, 16)
            total = jnp.zeros((16, HD), F32)
            for c0 in range(0, width, HD):
                total = total + hidden[rs, pl.ds(c0, HD)]
            mean = jnp.sum(total, axis=-1, keepdims=True) * (1.0 / width)
            mean = jnp.broadcast_to(mean, (16, HD))
            total = jnp.zeros((16, HD), F32)
            for c0 in range(0, width, HD):
                c = hidden[rs, pl.ds(c0, HD)] - mean
                total = total + c * c
            var = jnp.sum(total, axis=-1, keepdims=True) * (1.0 / width)
            rstd = jnp.broadcast_to(lax.rsqrt(var + EPS), (16, HD))
            for c0 in range(0, width, HD):
                cs = pl.ds(c0, HD)
                n = (hidden[rs, cs] - mean) * rstd
                scale = jnp.concatenate([scale_b[:, cs]] * 2, axis=0)
                shift = jnp.concatenate([shift_b[:, cs]] * 2, axis=0)
                normed[rs, cs] = (n * scale + shift).astype(BF16)

    def project(j, p):
        cols = pl.ds(p * pair_cols, pair_cols)
        dst = (q_s, k_s, v_s)[j]
        dst[:, cols] = jnp.dot(
            normed[...], w_qkv[j, :, cols], preferred_element_type=F32
        ).astype(dst.dtype)

    def norm_heads(src, dst):
        for h in range(heads):
            at = pl.ds(h * HD, HD)
            dst[:, at] = head_norm(src[:, at]).astype(BF16)

    factor = HD ** (-0.5) * math.log2(math.e)

    def score(h):
        at = pl.ds(h * HD, HD)
        q = q_n[:, at]
        own = lax.dot_general(q, k_n[:, at], NT, preferred_element_type=F32)
        far = jnp.dot(q, tk_t[at, :], preferred_element_type=F32)
        own = jnp.exp2(own * factor)
        far = jnp.exp2(far * factor)
        p_s[h, :, 0:rows] = own.astype(BF16)
        p_s[h, :, rows:keys] = far.astype(BF16)
        total = jnp.sum(own, axis=-1, keepdims=True) + jnp.sum(far, axis=-1, keepdims=True)
        l_s[h] = jnp.broadcast_to(total, (rows, HD))

    def weigh(h):
        at = pl.ds(h * HD, HD)
        mix = jnp.dot(p_s[h, :, 0:rows], v_s[:, at], preferred_element_type=F32)
        mix = mix + jnp.dot(p_s[h, :, rows:keys], tv[:, at], preferred_element_type=F32)
        att[:, at] = (mix / l_s[h]).astype(BF16)

    def text_head(h):
        at = pl.ds(h * HD, HD)
        tk_t[at, :] = jnp.transpose(head_norm(tk[:, at].astype(F32)).astype(BF16))

    def final_weights():
        mine = jnp.zeros((chan, HD), F32)
        other = jnp.zeros((chan, HD), F32)
        for c0 in range(0, half, HD):
            piece = w_fin[:, pl.ds(pl.multiple_of(half_at + c0, HD), HD)]
            w_fin_t[pl.ds(c0, HD), :] = jnp.transpose(jnp.concatenate([piece, piece], axis=0))
            mine = mine + piece.astype(F32)
            piece = w_fin[:, pl.ds(pl.multiple_of(half - half_at + c0, HD), HD)]
            other = other + piece.astype(F32)
        total = jnp.sum(mine - other, axis=-1, keepdims=True)
        total = jnp.broadcast_to(total, (chan, HD))
        cs_diff[...] = jnp.transpose(jnp.concatenate([total, total], axis=0))[0:8]

    offsets = sorted(range(1, steps), key=lambda o: abs(o - steps // 2))

    for sweep in range(ITERS):
        first = sweep == 0
        lat_move.start()
        if first:
            ld_in.wait()
            w_in2[chan : 2 * chan, :] = w_in2[0:chan, :]
        embed(0)
        if first:
            ld_ids.wait()
            ld_mod.wait()
            level = level_s[0]
            ones = jnp.ones((8, 1), F32)
            shift_b[...] = ones * mod_v[0, pl.ds(level, 1), :]
            scale_b[...] = ones * (1.0 + mod_v[1, pl.ds(level, 1), :])
        modulate(0)
        lat_move.wait_recv()
        embed(1)
        modulate(1)
        lat_move.wait_send()
        if first:
            for p in range(pairs):
                ld_qkv[p].wait()
                project(0, p)
                if p == 0:
                    ld_tk.wait()
                for h in (2 * p, 2 * p + 1):
                    text_head(h)
            norm_heads(q_s, q_n)
            for p in range(pairs):
                ld_qkv[pairs + p].wait()
                project(1, p)
                if p == 0:
                    ld_fin.wait()
                    final_weights()
            norm_heads(k_s, k_n)
            for h in range(heads):
                score(h)
            for p in range(pairs):
                ld_qkv[2 * pairs + p].wait()
                project(2, p)
            ld_tv.wait()
        else:
            for j in range(3):
                for p in range(pairs):
                    project(j, p)
            norm_heads(q_s, q_n)
            norm_heads(k_s, k_n)
            for h in range(heads):
                score(h)
        for p in range(pairs):
            for h in (2 * p, 2 * p + 1):
                weigh(h)
            for i in range(2):
                att_move(p, i).start()

        if first:
            ld_out[0].wait()
        for c0 in range(0, half, 512):
            cs = pl.ds(c0, 512)
            proj[:, cs] = jnp.dot(att[...], w_out[0, :, cs], preferred_element_type=F32)
        if first:
            ld_out[1].wait()
            ld_gate.wait()
            gate_b[...] = ones * gate_v[pl.ds(level, 1), :]
        for p in range(pairs):
            for i in range(2):
                att_move(p, i).wait()
        for c0 in range(0, half, 512):
            cs = pl.ds(c0, 512)
            from_par = jnp.dot(att_par[...], w_out[1, :, cs], preferred_element_type=F32)
            there = pl.ds(pl.multiple_of(half_at + c0, HD), 512)
            gate = gate_b[0:1, there]
            mixed[:, cs] = hidden[:, there] + gate * (proj[:, cs] + from_par)

        for r0 in range(0, rows, 16):
            rs = pl.ds(r0, 16)
            m = mixed[rs, :]
            mean = jnp.sum(m, axis=-1, keepdims=True) * (1.0 / half)
            c = m - mean
            square = jnp.sum(c * c, axis=-1, keepdims=True)
            centred[rs, :] = c.astype(BF16)
            dst = u_mine if r0 < tok else u_send
            ds = pl.ds(r0 % tok, 16)
            dst[1, ds, :] = jnp.broadcast_to(mean, (16, 2 * chan))
            dst[2, ds, :] = jnp.broadcast_to(square, (16, 2 * chan))
        u = jnp.dot(centred[...], w_fin_t[...], preferred_element_type=F32)
        u_mine[0] = u[0:tok]
        u_send[0] = u[tok:rows]
        if first:

            @pl.when(s == 0)
            def _():
                pl.semaphore_wait(barrier, steps - 1)

            ld_size.wait()
        u_move.start()
        u_move.wait()
        delta = (u_mine[1] - u_recv[1]) * 0.5
        var = (u_mine[2] + u_recv[2]) * (1.0 / width) + delta * delta
        velocity = u_mine[0] + u_recv[0] + delta * cs_diff[0:1, :]
        velocity = velocity * lax.rsqrt(var + EPS) * size_s[0]
        drift = jnp.where(low, velocity[0:pack], velocity[pack:tok])
        d_send[sweep] = drift.astype(BF16)

        def send_to(j):
            return pltpu.make_async_remote_copy(
                src_ref=d_send.at[sweep],
                dst_ref=d_recv.at[sweep, step],
                send_sem=d_send_sem.at[sweep],
                recv_sem=d_recv_sem.at[sweep, step],
                device_id=(j * groups + block, s),
                device_id_type=MESH,
            )

        for o in offsets:

            @pl.when(step + o < steps)
            def _():
                send_to(step + o).start()

        def take(j, total):
            pltpu.make_async_remote_copy(
                src_ref=d_send.at[sweep],
                dst_ref=d_recv.at[sweep, j],
                send_sem=d_send_sem.at[sweep],
                recv_sem=d_recv_sem.at[sweep, j],
                device_id=partner,
                device_id_type=MESH,
            ).wait_recv()
            return total + d_recv[sweep, j].astype(F32)

        earlier = lax.fori_loop(0, step, take, jnp.zeros((pack, 2 * chan), F32))
        if sweep < ITERS - 1:
            put_latent(noise_p[...] + earlier)
        else:
            final = noise_p[...] + (earlier + drift)
            out_ref[0:pack, :] = final[:, 0:chan]
            out_ref[pack:tok, :] = final[:, chan : 2 * chan]

    def sent(j, carry):
        for sweep in range(ITERS):
            pltpu.make_async_remote_copy(
                src_ref=d_send.at[sweep],
                dst_ref=d_recv.at[sweep, step],
                send_sem=d_send_sem.at[sweep],
                recv_sem=d_recv_sem.at[sweep, step],
                device_id=partner,
                device_id_type=MESH,
            ).wait_send()
        return carry

    lax.fori_loop(step + 1, steps, sent, 0)


def per_device(
    noise, step_size, step_ids, mod_table, w_in, w_qkv, w_out, w_final, text_keys, text_values
):
    groups, tok, chan = noise.shape
    steps = lax.axis_size("tm") // groups
    width = w_in.shape[1]
    half = width // 2
    txt, own_cols = text_keys.shape
    levels = mod_table.shape[0]
    heads = own_cols // HD
    pairs = heads // 2
    rows = 2 * tok
    pack = tok // 2
    hbm = pl.BlockSpec(memory_space=pltpu.HBM)
    vm = pltpu.VMEM
    dma = pltpu.SemaphoreType.DMA
    out = pl.pallas_call(
        functools.partial(kernel, groups, steps),
        out_shape=jax.ShapeDtypeStruct((tok, chan), F32),
        in_specs=[hbm] * 10,
        out_specs=pl.BlockSpec(memory_space=pltpu.VMEM),
        scratch_shapes=[
            pltpu.SMEM((1,), F32),
            pltpu.SMEM((1,), jnp.int32),
            vm((tok, chan), F32),
            vm((pack, 2 * chan), F32),
            vm((2, levels, width), F32),
            vm((levels, width), F32),
            vm((8, width), F32),
            vm((8, width), F32),
            vm((8, width), F32),
            vm((2 * chan, width), BF16),
            vm((3, width, own_cols), BF16),
            vm((2, own_cols, half), BF16),
            vm((chan, width), BF16),
            vm((half, 2 * chan), BF16),
            vm((8, 2 * chan), F32),
            vm((txt, own_cols), BF16),
            vm((txt, own_cols), BF16),
            vm((own_cols, txt), BF16),
            vm((rows, 2 * chan), BF16),
            vm((rows, width), F32),
            vm((rows, width), BF16),
            vm((rows, own_cols), F32),
            vm((rows, own_cols), F32),
            vm((rows, own_cols), BF16),
            vm((rows, own_cols), BF16),
            vm((rows, own_cols), BF16),
            vm((heads, rows, rows + txt), BF16),
            vm((heads, rows, HD), F32),
            vm((rows, own_cols), BF16),
            vm((rows, own_cols), BF16),
            vm((rows, half), F32),
            vm((rows, half), F32),
            vm((rows, half), BF16),
            vm((3, tok, 2 * chan), F32),
            vm((3, tok, 2 * chan), F32),
            vm((3, tok, 2 * chan), F32),
            vm((ITERS, pack, 2 * chan), BF16),
            vm((ITERS, steps, pack, 2 * chan), BF16),
            dma((24,)),
            pltpu.SemaphoreType.REGULAR,
            dma((2,)),
            dma((2, pairs, 2)),
            dma((2,)),
            dma((ITERS,)),
            dma((ITERS, steps)),
        ],
        compiler_params=pltpu.CompilerParams(
            collective_id=0, has_side_effects=True, vmem_limit_bytes=56 * 2**20
        ),
        cost_estimate=pl.CostEstimate(
            flops=5 * 10**9, bytes_accessed=25 * 10**6, transcendentals=10**6
        ),
        name="picard",
    )(
        step_size,
        step_ids,
        noise,
        jnp.transpose(mod_table, (1, 0, 2)),
        w_in,
        jnp.transpose(w_qkv, (1, 0, 2)),
        w_out,
        jnp.transpose(w_final, (1, 0)),
        text_keys,
        text_values,
    )
    return out[None]


def solution(mesh):
    placed = (
        P(None, "seq", None),
        P("tm"),
        P("tm"),
        P(),
        P(),
        P(None, None, "seq"),
        P(),
        P(),
        P(None, "seq"),
        P(None, "seq"),
    )
    return jax.shard_map(
        per_device, mesh=mesh, in_specs=placed, out_specs=P("tm", "seq", None), check_vma=False
    )
```

```python
import functools
import math

import jax
import jax.numpy as jnp
from jax import lax
from jax.experimental import pallas as pl
from jax.experimental.pallas import tpu as pltpu
from jax.sharding import PartitionSpec as P

HD = 128
ITERS = 2
EPS = 1e-06
MESH = pl.DeviceIdType.MESH
F32 = jnp.float32
BF16 = jnp.bfloat16
NT = (((1,), (1,)), ((), ()))


def head_norm(values):
    return values * lax.rsqrt(jnp.mean(values * values, axis=-1, keepdims=True) + EPS)


def kernel(
    groups,
    steps,
    step_size_hbm,
    step_ids_hbm,
    noise_hbm,
    mod_hbm,
    w_in_hbm,
    w_qkv_hbm,
    w_out_hbm,
    w_fin_hbm,
    tk_hbm,
    tv_hbm,
    out_ref,
    size_s,
    level_s,
    noise_raw,
    noise_p,
    mod_v,
    gate_v,
    shift_b,
    scale_b,
    gate_b,
    w_in2,
    w_qkv,
    w_out,
    w_fin,
    w_fin_t,
    cs_diff,
    tk,
    tv,
    tk_t,
    lat,
    hidden,
    normed,
    q_s,
    k_s,
    v_s,
    q_n,
    k_n,
    p_s,
    l_s,
    att,
    att_par,
    proj,
    mixed,
    centred,
    u_mine,
    u_send,
    u_recv,
    d_send,
    d_recv,
    load_sem,
    in_sem,
    lat_sem,
    att_sem,
    u_sem,
    d_send_sem,
    d_recv_sem,
):
    tok, chan = noise_raw.shape
    width = hidden.shape[1]
    half = width // 2
    own_cols = w_qkv.shape[2]
    heads = own_cols // HD
    pair_cols = 2 * HD
    pairs = own_cols // pair_cols
    txt = tk.shape[0]
    rows = 2 * tok
    keys = rows + txt
    pack = tok // 2

    t = lax.axis_index("tm")
    s = lax.axis_index("seq")
    block = lax.rem(t, groups)
    step = t // groups
    partner = (t, 1 - s)

    barrier = pltpu.get_barrier_semaphore()

    @pl.when(s == 0)
    def _():
        pl.semaphore_signal(barrier, inc=1, device_id=partner, device_id_type=MESH)

    counter = iter(range(64))

    def load(src, dst):
        copy = pltpu.make_async_copy(src, dst, load_sem.at[next(counter)])
        copy.start()
        return copy

    half_at = pl.multiple_of(s * half, HD)
    ld_noise = load(noise_hbm.at[block], noise_raw)
    ld_ids = load(step_ids_hbm, level_s)
    ld_size = load(step_size_hbm, size_s)
    ld_in = load(w_in_hbm, w_in2.at[pl.ds(0, chan)])
    ld_mod = load(mod_hbm.at[pl.ds(0, 2)], mod_v)
    ld_tk = load(tk_hbm, tk)
    ld_qkv = []
    for j in range(3):
        if j == 1:
            ld_fin = load(w_fin_hbm, w_fin)
        if j == 2:
            ld_tv = load(tv_hbm, tv)
            ld_gate = load(mod_hbm.at[2], gate_v)
        for p in range(pairs):
            cols = pl.ds(p * pair_cols, pair_cols)
            ld_qkv.append(load(w_qkv_hbm.at[j, :, cols], w_qkv.at[j, :, cols]))
    ld_out = []

    def load_out():
        for i in range(2):
            at = pl.multiple_of((s if i == 0 else 1 - s) * own_cols, HD)
            ld_out.append(
                load(w_out_hbm.at[pl.ds(at, own_cols), pl.ds(half_at, half)], w_out.at[i])
            )

    @pl.when(s == 1)
    def _():
        pl.semaphore_wait(barrier, 1)
        pl.semaphore_signal(in_sem, inc=1, device_id=partner, device_id_type=MESH)

    @pl.when(s == 0)
    def _():
        pl.semaphore_wait(in_sem, 1)

        def greet(j, carry):
            @pl.when(j != step)
            def _():
                pl.semaphore_signal(
                    barrier, inc=1, device_id=(j * groups + block, 0), device_id_type=MESH
                )

            return carry

        lax.fori_loop(0, steps, greet, 0)

    lane = lax.broadcasted_iota(jnp.int32, (pack, 2 * chan), 1)
    low = lane < chan

    def put_latent(packed):
        lat[0:pack, :] = jnp.where(low, packed, 0.0).astype(BF16)
        lat[pack:tok, :] = jnp.where(low, 0.0, packed).astype(BF16)

    ld_noise.wait()
    raw = noise_raw[...]
    noise_p[...] = jnp.concatenate([raw[0:pack], raw[pack:tok]], axis=1)
    put_latent(noise_p[...])

    lat_move = pltpu.make_async_remote_copy(
        src_ref=lat.at[pl.ds(0, tok)],
        dst_ref=lat.at[pl.ds(tok, tok)],
        send_sem=lat_sem.at[0],
        recv_sem=lat_sem.at[1],
        device_id=partner,
        device_id_type=MESH,
    )

    def att_move(p, i):
        cols = pl.ds(p * pair_cols, pair_cols)
        return pltpu.make_async_remote_copy(
            src_ref=att.at[pl.ds(i * tok, tok), cols],
            dst_ref=att_par.at[pl.ds((1 - i) * tok, tok), cols],
            send_sem=att_sem.at[0, p, i],
            recv_sem=att_sem.at[1, p, i],
            device_id=partner,
            device_id_type=MESH,
        )

    u_move = pltpu.make_async_remote_copy(
        src_ref=u_send,
        dst_ref=u_recv,
        send_sem=u_sem.at[0],
        recv_sem=u_sem.at[1],
        device_id=partner,
        device_id_type=MESH,
    )

    def embed(part):
        at = pl.ds(part * tok, tok)
        for c0 in range(0, width, 512):
            cs = pl.ds(c0, 512)
            hidden[at, cs] = jnp.dot(lat[at, :], w_in2[:, cs], preferred_element_type=F32)

    def modulate(part):
        for r0 in range(part * tok, part * tok + tok, 16):
            rs = pl.ds(r0, 16)
            total = jnp.zeros((16, HD), F32)
            for c0 in range(0, width, HD):
                total = total + hidden[rs, pl.ds(c0, HD)]
            mean = jnp.sum(total, axis=-1, keepdims=True) * (1.0 / width)
            mean = jnp.broadcast_to(mean, (16, HD))
            total = jnp.zeros((16, HD), F32)
            for c0 in range(0, width, HD):
                c = hidden[rs, pl.ds(c0, HD)] - mean
                total = total + c * c
            var = jnp.sum(total, axis=-1, keepdims=True) * (1.0 / width)
            rstd = jnp.broadcast_to(lax.rsqrt(var + EPS), (16, HD))
            for c0 in range(0, width, HD):
                cs = pl.ds(c0, HD)
                n = (hidden[rs, cs] - mean) * rstd
                scale = jnp.concatenate([scale_b[:, cs]] * 2, axis=0)
                shift = jnp.concatenate([shift_b[:, cs]] * 2, axis=0)
                normed[rs, cs] = (n * scale + shift).astype(BF16)

    def project(j, p):
        cols = pl.ds(p * pair_cols, pair_cols)
        dst = (q_s, k_s, v_s)[j]
        dst[:, cols] = jnp.dot(
            normed[...], w_qkv[j, :, cols], preferred_element_type=F32
        ).astype(dst.dtype)

    def norm_heads(src, dst):
        for h in range(heads):
            at = pl.ds(h * HD, HD)
            dst[:, at] = head_norm(src[:, at]).astype(BF16)

    factor = HD ** (-0.5) * math.log2(math.e)

    def score(h):
        at = pl.ds(h * HD, HD)
        q = q_n[:, at]
        own = lax.dot_general(q, k_n[:, at], NT, preferred_element_type=F32)
        far = jnp.dot(q, tk_t[at, :], preferred_element_type=F32)
        own = jnp.exp2(own * factor)
        far = jnp.exp2(far * factor)
        p_s[h, :, 0:rows] = own.astype(BF16)
        p_s[h, :, rows:keys] = far.astype(BF16)
        total = jnp.sum(own, axis=-1, keepdims=True) + jnp.sum(far, axis=-1, keepdims=True)
        l_s[h] = jnp.broadcast_to(total, (rows, HD))

    def weigh(h):
        at = pl.ds(h * HD, HD)
        mix = jnp.dot(p_s[h, :, 0:rows], v_s[:, at], preferred_element_type=F32)
        mix = mix + jnp.dot(p_s[h, :, rows:keys], tv[:, at], preferred_element_type=F32)
        att[:, at] = (mix / l_s[h]).astype(BF16)

    def text_head(h):
        at = pl.ds(h * HD, HD)
        tk_t[at, :] = jnp.transpose(head_norm(tk[:, at].astype(F32)).astype(BF16))

    def final_weights():
        mine = jnp.zeros((chan, HD), F32)
        other = jnp.zeros((chan, HD), F32)
        for c0 in range(0, half, HD):
            piece = w_fin[:, pl.ds(pl.multiple_of(half_at + c0, HD), HD)]
            w_fin_t[pl.ds(c0, HD), :] = jnp.transpose(jnp.concatenate([piece, piece], axis=0))
            mine = mine + piece.astype(F32)
            piece = w_fin[:, pl.ds(pl.multiple_of(half - half_at + c0, HD), HD)]
            other = other + piece.astype(F32)
        total = jnp.sum(mine - other, axis=-1, keepdims=True)
        total = jnp.broadcast_to(total, (chan, HD))
        cs_diff[...] = jnp.transpose(jnp.concatenate([total, total], axis=0))[0:8]

    offsets = sorted(range(1, steps), key=lambda o: abs(o - steps // 2))

    for sweep in range(ITERS):
        first = sweep == 0
        lat_move.start()
        if first:
            ld_in.wait()
            w_in2[chan : 2 * chan, :] = w_in2[0:chan, :]
        embed(0)
        if first:
            ld_ids.wait()
            ld_mod.wait()
            level = level_s[0]
            ones = jnp.ones((8, 1), F32)
            shift_b[...] = ones * mod_v[0, pl.ds(level, 1), :]
            scale_b[...] = ones * (1.0 + mod_v[1, pl.ds(level, 1), :])
        modulate(0)
        lat_move.wait_recv()
        embed(1)
        modulate(1)
        lat_move.wait_send()
        for j in range(3):
            if first and j < 2:
                for p in range(pairs):
                    ld_qkv[j * pairs + p].wait()
            for p in range(pairs):
                if first and j == 2:
                    ld_qkv[j * pairs + p].wait()
                project(j, p)
            if first and j == 0:
                load_out()
                ld_tk.wait()
                for h in range(heads):
                    text_head(h)
            if first and j == 1:
                ld_fin.wait()
                final_weights()
            if j == (1 if first else 2):
                norm_heads(q_s, q_n)
                norm_heads(k_s, k_n)
                for h in range(heads):
                    score(h)
        if first:
            ld_tv.wait()
        for p in range(pairs):
            for h in (2 * p, 2 * p + 1):
                weigh(h)
            for i in range(2):
                att_move(p, i).start()

        if first:
            ld_out[0].wait()
        for c0 in range(0, half, 512):
            cs = pl.ds(c0, 512)
            proj[:, cs] = jnp.dot(att[...], w_out[0, :, cs], preferred_element_type=F32)
        if first:
            ld_out[1].wait()
            ld_gate.wait()
            gate_b[...] = ones * gate_v[pl.ds(level, 1), :]
        for p in range(pairs):
            for i in range(2):
                att_move(p, i).wait()
        for c0 in range(0, half, 512):
            cs = pl.ds(c0, 512)
            from_par = jnp.dot(att_par[...], w_out[1, :, cs], preferred_element_type=F32)
            there = pl.ds(pl.multiple_of(half_at + c0, HD), 512)
            gate = gate_b[0:1, there]
            mixed[:, cs] = hidden[:, there] + gate * (proj[:, cs] + from_par)

        for r0 in range(0, rows, 16):
            rs = pl.ds(r0, 16)
            m = mixed[rs, :]
            mean = jnp.sum(m, axis=-1, keepdims=True) * (1.0 / half)
            c = m - mean
            square = jnp.sum(c * c, axis=-1, keepdims=True)
            centred[rs, :] = c.astype(BF16)
            dst = u_mine if r0 < tok else u_send
            ds = pl.ds(r0 % tok, 16)
            dst[1, ds, :] = jnp.broadcast_to(mean, (16, 2 * chan))
            dst[2, ds, :] = jnp.broadcast_to(square, (16, 2 * chan))
        u = jnp.dot(centred[...], w_fin_t[...], preferred_element_type=F32)
        u_mine[0] = u[0:tok]
        u_send[0] = u[tok:rows]
        if first:

            @pl.when(s == 0)
            def _():
                pl.semaphore_wait(barrier, steps - 1)

            ld_size.wait()
        u_move.start()
        u_move.wait()
        delta = (u_mine[1] - u_recv[1]) * 0.5
        var = (u_mine[2] + u_recv[2]) * (1.0 / width) + delta * delta
        velocity = u_mine[0] + u_recv[0] + delta * cs_diff[0:1, :]
        velocity = velocity * lax.rsqrt(var + EPS) * size_s[0]
        drift = jnp.where(low, velocity[0:pack], velocity[pack:tok])
        d_send[sweep] = drift.astype(BF16)

        def send_to(j):
            return pltpu.make_async_remote_copy(
                src_ref=d_send.at[sweep],
                dst_ref=d_recv.at[sweep, step],
                send_sem=d_send_sem.at[sweep],
                recv_sem=d_recv_sem.at[sweep, step],
                device_id=(j * groups + block, s),
                device_id_type=MESH,
            )

        for o in offsets:

            @pl.when(step + o < steps)
            def _():
                send_to(step + o).start()

        def take(j, total):
            pltpu.make_async_remote_copy(
                src_ref=d_send.at[sweep],
                dst_ref=d_recv.at[sweep, j],
                send_sem=d_send_sem.at[sweep],
                recv_sem=d_recv_sem.at[sweep, j],
                device_id=partner,
                device_id_type=MESH,
            ).wait_recv()
            return total + d_recv[sweep, j].astype(F32)

        earlier = lax.fori_loop(0, step, take, jnp.zeros((pack, 2 * chan), F32))
        if sweep < ITERS - 1:
            put_latent(noise_p[...] + earlier)
        else:
            final = noise_p[...] + (earlier + drift)
            out_ref[0:pack, :] = final[:, 0:chan]
            out_ref[pack:tok, :] = final[:, chan : 2 * chan]

    def sent(j, carry):
        for sweep in range(ITERS):
            pltpu.make_async_remote_copy(
                src_ref=d_send.at[sweep],
                dst_ref=d_recv.at[sweep, step],
                send_sem=d_send_sem.at[sweep],
                recv_sem=d_recv_sem.at[sweep, step],
                device_id=partner,
                device_id_type=MESH,
            ).wait_send()
        return carry

    lax.fori_loop(step + 1, steps, sent, 0)


def per_device(
    noise, step_size, step_ids, mod_table, w_in, w_qkv, w_out, w_final, text_keys, text_values
):
    groups, tok, chan = noise.shape
    steps = lax.axis_size("tm") // groups
    width = w_in.shape[1]
    half = width // 2
    txt, own_cols = text_keys.shape
    levels = mod_table.shape[0]
    heads = own_cols // HD
    pairs = heads // 2
    rows = 2 * tok
    pack = tok // 2
    hbm = pl.BlockSpec(memory_space=pltpu.HBM)
    vm = pltpu.VMEM
    dma = pltpu.SemaphoreType.DMA
    out = pl.pallas_call(
        functools.partial(kernel, groups, steps),
        out_shape=jax.ShapeDtypeStruct((tok, chan), F32),
        in_specs=[hbm] * 10,
        out_specs=pl.BlockSpec(memory_space=pltpu.VMEM),
        scratch_shapes=[
            pltpu.SMEM((1,), F32),
            pltpu.SMEM((1,), jnp.int32),
            vm((tok, chan), F32),
            vm((pack, 2 * chan), F32),
            vm((2, levels, width), F32),
            vm((levels, width), F32),
            vm((8, width), F32),
            vm((8, width), F32),
            vm((8, width), F32),
            vm((2 * chan, width), BF16),
            vm((3, width, own_cols), BF16),
            vm((2, own_cols, half), BF16),
            vm((chan, width), BF16),
            vm((half, 2 * chan), BF16),
            vm((8, 2 * chan), F32),
            vm((txt, own_cols), BF16),
            vm((txt, own_cols), BF16),
            vm((own_cols, txt), BF16),
            vm((rows, 2 * chan), BF16),
            vm((rows, width), F32),
            vm((rows, width), BF16),
            vm((rows, own_cols), F32),
            vm((rows, own_cols), F32),
            vm((rows, own_cols), BF16),
            vm((rows, own_cols), BF16),
            vm((rows, own_cols), BF16),
            vm((heads, rows, rows + txt), BF16),
            vm((heads, rows, HD), F32),
            vm((rows, own_cols), BF16),
            vm((rows, own_cols), BF16),
            vm((rows, half), F32),
            vm((rows, half), F32),
            vm((rows, half), BF16),
            vm((3, tok, 2 * chan), F32),
            vm((3, tok, 2 * chan), F32),
            vm((3, tok, 2 * chan), F32),
            vm((ITERS, pack, 2 * chan), BF16),
            vm((ITERS, steps, pack, 2 * chan), BF16),
            dma((24,)),
            pltpu.SemaphoreType.REGULAR,
            dma((2,)),
            dma((2, pairs, 2)),
            dma((2,)),
            dma((ITERS,)),
            dma((ITERS, steps)),
        ],
        compiler_params=pltpu.CompilerParams(
            collective_id=0, has_side_effects=True, vmem_limit_bytes=55193 * 1024
        ),
        cost_estimate=pl.CostEstimate(
            flops=5 * 10**9, bytes_accessed=25 * 10**6, transcendentals=10**6
        ),
        name="picard",
    )(
        step_size,
        step_ids,
        noise,
        jnp.transpose(mod_table, (1, 0, 2)),
        w_in,
        jnp.transpose(w_qkv, (1, 0, 2)),
        w_out,
        jnp.transpose(w_final, (1, 0)),
        text_keys,
        text_values,
    )
    return out[None]


def solution(mesh):
    placed = (
        P(None, "seq", None),
        P("tm"),
        P("tm"),
        P(),
        P(),
        P(None, None, "seq"),
        P(),
        P(),
        P(None, "seq"),
        P(None, "seq"),
    )
    return jax.shard_map(
        per_device, mesh=mesh, in_specs=placed, out_specs=P("tm", "seq", None), check_vma=False
    )
```

```python
import functools
import math

import jax
import jax.numpy as jnp
from jax import lax
from jax.experimental import pallas as pl
from jax.experimental.pallas import tpu as pltpu
from jax.sharding import PartitionSpec as P

HD = 128
ITERS = 2
EPS = 1e-06
MESH = pl.DeviceIdType.MESH
F32 = jnp.float32
BF16 = jnp.bfloat16
NT = (((1,), (1,)), ((), ()))


def head_norm(values):
    return values * lax.rsqrt(jnp.mean(values * values, axis=-1, keepdims=True) + EPS)


def kernel(
    groups,
    steps,
    step_size_hbm,
    step_ids_hbm,
    noise_hbm,
    mod_hbm,
    w_in_hbm,
    w_qkv_hbm,
    w_out_hbm,
    w_fin_hbm,
    tk_hbm,
    tv_hbm,
    out_ref,
    size_s,
    level_s,
    noise_raw,
    noise_p,
    mod_v,
    gate_v,
    shift_b,
    scale_b,
    gate_b,
    w_in2,
    w_qkv,
    w_out,
    w_fin,
    w_fin_t,
    cs_diff,
    tk,
    tv,
    tk_t,
    lat,
    hidden,
    normed,
    q_s,
    k_s,
    v_s,
    q_n,
    k_n,
    p_s,
    l_s,
    att,
    att_par,
    proj,
    mixed,
    centred,
    u_mine,
    u_send,
    u_recv,
    d_send,
    d_recv,
    load_sem,
    in_sem,
    lat_sem,
    att_sem,
    u_sem,
    d_send_sem,
    d_recv_sem,
):
    tok, chan = noise_raw.shape
    width = hidden.shape[1]
    half = width // 2
    own_cols = w_qkv.shape[2]
    heads = own_cols // HD
    pair_cols = 2 * HD
    pairs = own_cols // pair_cols
    txt = tk.shape[0]
    rows = 2 * tok
    keys = rows + txt
    pack = tok // 2

    t = lax.axis_index("tm")
    s = lax.axis_index("seq")
    block = lax.rem(t, groups)
    step = t // groups
    partner = (t, 1 - s)

    barrier = pltpu.get_barrier_semaphore()

    @pl.when(s == 0)
    def _():
        pl.semaphore_signal(barrier, inc=1, device_id=partner, device_id_type=MESH)

    counter = iter(range(64))

    def load(src, dst):
        copy = pltpu.make_async_copy(src, dst, load_sem.at[next(counter)])
        copy.start()
        return copy

    half_at = pl.multiple_of(s * half, HD)
    ld_noise = load(noise_hbm.at[block], noise_raw)
    ld_ids = load(step_ids_hbm, level_s)
    ld_size = load(step_size_hbm, size_s)
    ld_in = load(w_in_hbm, w_in2.at[pl.ds(0, chan)])
    ld_mod = load(mod_hbm.at[pl.ds(0, 2)], mod_v)
    ld_tk = load(tk_hbm, tk)
    ld_fin = load(w_fin_hbm, w_fin)
    ld_qkv = []
    for j in range(3):
        if j == 2:
            ld_tv = load(tv_hbm, tv)
            ld_gate = load(mod_hbm.at[2], gate_v)
        for p in range(pairs):
            cols = pl.ds(p * pair_cols, pair_cols)
            ld_qkv.append(load(w_qkv_hbm.at[j, :, cols], w_qkv.at[j, :, cols]))
    ld_out = []

    def load_out():
        for i in range(2):
            at = pl.multiple_of((s if i == 0 else 1 - s) * own_cols, HD)
            ld_out.append(
                load(w_out_hbm.at[pl.ds(at, own_cols), pl.ds(half_at, half)], w_out.at[i])
            )

    @pl.when(s == 1)
    def _():
        pl.semaphore_wait(barrier, 1)
        pl.semaphore_signal(in_sem, inc=1, device_id=partner, device_id_type=MESH)

    @pl.when(s == 0)
    def _():
        pl.semaphore_wait(in_sem, 1)

        def greet(j, carry):
            @pl.when(j != step)
            def _():
                pl.semaphore_signal(
                    barrier, inc=1, device_id=(j * groups + block, 0), device_id_type=MESH
                )

            return carry

        lax.fori_loop(0, steps, greet, 0)

    lane = lax.broadcasted_iota(jnp.int32, (pack, 2 * chan), 1)
    low = lane < chan

    def put_latent(packed):
        lat[0:pack, :] = jnp.where(low, packed, 0.0).astype(BF16)
        lat[pack:tok, :] = jnp.where(low, 0.0, packed).astype(BF16)

    ld_noise.wait()
    raw = noise_raw[...]
    noise_p[...] = jnp.concatenate([raw[0:pack], raw[pack:tok]], axis=1)
    put_latent(noise_p[...])

    lat_move = pltpu.make_async_remote_copy(
        src_ref=lat.at[pl.ds(0, tok)],
        dst_ref=lat.at[pl.ds(tok, tok)],
        send_sem=lat_sem.at[0],
        recv_sem=lat_sem.at[1],
        device_id=partner,
        device_id_type=MESH,
    )

    def att_move(p, i):
        cols = pl.ds(p * pair_cols, pair_cols)
        return pltpu.make_async_remote_copy(
            src_ref=att.at[pl.ds(i * tok, tok), cols],
            dst_ref=att_par.at[pl.ds((1 - i) * tok, tok), cols],
            send_sem=att_sem.at[0, p, i],
            recv_sem=att_sem.at[1, p, i],
            device_id=partner,
            device_id_type=MESH,
        )

    u_move = pltpu.make_async_remote_copy(
        src_ref=u_send,
        dst_ref=u_recv,
        send_sem=u_sem.at[0],
        recv_sem=u_sem.at[1],
        device_id=partner,
        device_id_type=MESH,
    )

    def embed(part):
        at = pl.ds(part * tok, tok)
        for c0 in range(0, width, 512):
            cs = pl.ds(c0, 512)
            hidden[at, cs] = jnp.dot(lat[at, :], w_in2[:, cs], preferred_element_type=F32)

    def modulate(part):
        for r0 in range(part * tok, part * tok + tok, 16):
            rs = pl.ds(r0, 16)
            total = jnp.zeros((16, HD), F32)
            for c0 in range(0, width, HD):
                total = total + hidden[rs, pl.ds(c0, HD)]
            mean = jnp.sum(total, axis=-1, keepdims=True) * (1.0 / width)
            mean = jnp.broadcast_to(mean, (16, HD))
            total = jnp.zeros((16, HD), F32)
            for c0 in range(0, width, HD):
                c = hidden[rs, pl.ds(c0, HD)] - mean
                total = total + c * c
            var = jnp.sum(total, axis=-1, keepdims=True) * (1.0 / width)
            rstd = jnp.broadcast_to(lax.rsqrt(var + EPS), (16, HD))
            for c0 in range(0, width, HD):
                cs = pl.ds(c0, HD)
                n = (hidden[rs, cs] - mean) * rstd
                scale = jnp.concatenate([scale_b[:, cs]] * 2, axis=0)
                shift = jnp.concatenate([shift_b[:, cs]] * 2, axis=0)
                normed[rs, cs] = (n * scale + shift).astype(BF16)

    def project(j, p):
        cols = pl.ds(p * pair_cols, pair_cols)
        dst = (q_s, k_s, v_s)[j]
        dst[:, cols] = jnp.dot(
            normed[...], w_qkv[j, :, cols], preferred_element_type=F32
        ).astype(dst.dtype)

    def norm_heads(src, dst):
        for h in range(heads):
            at = pl.ds(h * HD, HD)
            dst[:, at] = head_norm(src[:, at]).astype(BF16)

    factor = HD ** (-0.5) * math.log2(math.e)

    def score(h):
        at = pl.ds(h * HD, HD)
        q = q_n[:, at]
        own = lax.dot_general(q, k_n[:, at], NT, preferred_element_type=F32)
        far = jnp.dot(q, tk_t[at, :], preferred_element_type=F32)
        own = jnp.exp2(own * factor)
        far = jnp.exp2(far * factor)
        p_s[h, :, 0:rows] = own.astype(BF16)
        p_s[h, :, rows:keys] = far.astype(BF16)
        total = jnp.sum(own, axis=-1, keepdims=True) + jnp.sum(far, axis=-1, keepdims=True)
        l_s[h] = jnp.broadcast_to(total, (rows, HD))

    def weigh(h):
        at = pl.ds(h * HD, HD)
        mix = jnp.dot(p_s[h, :, 0:rows], v_s[:, at], preferred_element_type=F32)
        mix = mix + jnp.dot(p_s[h, :, rows:keys], tv[:, at], preferred_element_type=F32)
        att[:, at] = (mix / l_s[h]).astype(BF16)

    def text_head(h):
        at = pl.ds(h * HD, HD)
        tk_t[at, :] = jnp.transpose(head_norm(tk[:, at].astype(F32)).astype(BF16))

    def final_weights():
        mine = jnp.zeros((chan, HD), F32)
        other = jnp.zeros((chan, HD), F32)
        for c0 in range(0, half, HD):
            piece = w_fin[:, pl.ds(pl.multiple_of(half_at + c0, HD), HD)]
            w_fin_t[pl.ds(c0, HD), :] = jnp.transpose(jnp.concatenate([piece, piece], axis=0))
            mine = mine + piece.astype(F32)
            piece = w_fin[:, pl.ds(pl.multiple_of(half - half_at + c0, HD), HD)]
            other = other + piece.astype(F32)
        total = jnp.sum(mine - other, axis=-1, keepdims=True)
        total = jnp.broadcast_to(total, (chan, HD))
        cs_diff[...] = jnp.transpose(jnp.concatenate([total, total], axis=0))[0:8]

    offsets = sorted(range(1, steps), key=lambda o: abs(o - steps // 2))

    for sweep in range(ITERS):
        first = sweep == 0
        lat_move.start()
        if first:
            ld_in.wait()
            w_in2[chan : 2 * chan, :] = w_in2[0:chan, :]
        embed(0)
        if first:
            ld_ids.wait()
            ld_mod.wait()
            level = level_s[0]
            ones = jnp.ones((8, 1), F32)
            shift_b[...] = ones * mod_v[0, pl.ds(level, 1), :]
            scale_b[...] = ones * (1.0 + mod_v[1, pl.ds(level, 1), :])
        modulate(0)
        lat_move.wait_recv()
        embed(1)
        modulate(1)
        lat_move.wait_send()
        if first:
            ld_tk.wait()
            for h in range(heads):
                text_head(h)
            ld_fin.wait()
            final_weights()
        for j in range(3):
            if first:
                for p in range(pairs):
                    ld_qkv[j * pairs + p].wait()
            for p in range(pairs):
                project(j, p)
            if first and j == 0:
                load_out()
                norm_heads(q_s, q_n)
            if j == (1 if first else 2):
                if not first:
                    norm_heads(q_s, q_n)
                norm_heads(k_s, k_n)
                for h in range(heads):
                    score(h)
        if first:
            ld_tv.wait()
        for p in range(pairs):
            for h in (2 * p, 2 * p + 1):
                weigh(h)
            for i in range(2):
                att_move(p, i).start()

        if first:
            ld_out[0].wait()
        for c0 in range(0, half, 512):
            cs = pl.ds(c0, 512)
            proj[:, cs] = jnp.dot(att[...], w_out[0, :, cs], preferred_element_type=F32)
        if first:
            ld_out[1].wait()
            ld_gate.wait()
            gate_b[...] = ones * gate_v[pl.ds(level, 1), :]
        for p in range(pairs):
            for i in range(2):
                att_move(p, i).wait()
        for c0 in range(0, half, 512):
            cs = pl.ds(c0, 512)
            from_par = jnp.dot(att_par[...], w_out[1, :, cs], preferred_element_type=F32)
            there = pl.ds(pl.multiple_of(half_at + c0, HD), 512)
            gate = gate_b[0:1, there]
            mixed[:, cs] = hidden[:, there] + gate * (proj[:, cs] + from_par)

        for part in (1, 0):
            dst = (u_mine, u_send)[part]
            for r0 in range(0, tok, 16):
                rs = pl.ds(part * tok + r0, 16)
                m = mixed[rs, :]
                mean = jnp.sum(m, axis=-1, keepdims=True) * (1.0 / half)
                c = m - mean
                square = jnp.sum(c * c, axis=-1, keepdims=True)
                centred[rs, :] = c.astype(BF16)
                ds = pl.ds(r0, 16)
                dst[1, ds, :] = jnp.broadcast_to(mean, (16, 2 * chan))
                dst[2, ds, :] = jnp.broadcast_to(square, (16, 2 * chan))
            dst[0] = jnp.dot(
                centred[pl.ds(part * tok, tok), :], w_fin_t[...], preferred_element_type=F32
            )
            if part == 1:
                if first:

                    @pl.when(s == 0)
                    def _():
                        pl.semaphore_wait(barrier, steps - 1)

                    ld_size.wait()
                u_move.start()
        u_move.wait()
        delta = (u_mine[1] - u_recv[1]) * 0.5
        var = (u_mine[2] + u_recv[2]) * (1.0 / width) + delta * delta
        velocity = u_mine[0] + u_recv[0] + delta * cs_diff[0:1, :]
        velocity = velocity * lax.rsqrt(var + EPS) * size_s[0]
        drift = jnp.where(low, velocity[0:pack], velocity[pack:tok])
        d_send[sweep] = drift.astype(BF16)

        def send_to(j):
            return pltpu.make_async_remote_copy(
                src_ref=d_send.at[sweep],
                dst_ref=d_recv.at[sweep, step],
                send_sem=d_send_sem.at[sweep],
                recv_sem=d_recv_sem.at[sweep, step],
                device_id=(j * groups + block, s),
                device_id_type=MESH,
            )

        for o in offsets:

            @pl.when(step + o < steps)
            def _():
                send_to(step + o).start()

        def take(j, total):
            pltpu.make_async_remote_copy(
                src_ref=d_send.at[sweep],
                dst_ref=d_recv.at[sweep, j],
                send_sem=d_send_sem.at[sweep],
                recv_sem=d_recv_sem.at[sweep, j],
                device_id=partner,
                device_id_type=MESH,
            ).wait_recv()
            return total + d_recv[sweep, j].astype(F32)

        earlier = lax.fori_loop(0, step, take, jnp.zeros((pack, 2 * chan), F32))
        if sweep < ITERS - 1:
            put_latent(noise_p[...] + earlier)
        else:
            final = noise_p[...] + (earlier + drift)
            out_ref[0:pack, :] = final[:, 0:chan]
            out_ref[pack:tok, :] = final[:, chan : 2 * chan]

    def sent(j, carry):
        for sweep in range(ITERS):
            pltpu.make_async_remote_copy(
                src_ref=d_send.at[sweep],
                dst_ref=d_recv.at[sweep, step],
                send_sem=d_send_sem.at[sweep],
                recv_sem=d_recv_sem.at[sweep, step],
                device_id=partner,
                device_id_type=MESH,
            ).wait_send()
        return carry

    lax.fori_loop(step + 1, steps, sent, 0)


def per_device(
    noise, step_size, step_ids, mod_table, w_in, w_qkv, w_out, w_final, text_keys, text_values
):
    groups, tok, chan = noise.shape
    steps = lax.axis_size("tm") // groups
    width = w_in.shape[1]
    half = width // 2
    txt, own_cols = text_keys.shape
    levels = mod_table.shape[0]
    heads = own_cols // HD
    pairs = heads // 2
    rows = 2 * tok
    pack = tok // 2
    hbm = pl.BlockSpec(memory_space=pltpu.HBM)
    vm = pltpu.VMEM
    dma = pltpu.SemaphoreType.DMA
    out = pl.pallas_call(
        functools.partial(kernel, groups, steps),
        out_shape=jax.ShapeDtypeStruct((tok, chan), F32),
        in_specs=[hbm] * 10,
        out_specs=pl.BlockSpec(memory_space=pltpu.VMEM),
        scratch_shapes=[
            pltpu.SMEM((1,), F32),
            pltpu.SMEM((1,), jnp.int32),
            vm((tok, chan), F32),
            vm((pack, 2 * chan), F32),
            vm((2, levels, width), F32),
            vm((levels, width), F32),
            vm((8, width), F32),
            vm((8, width), F32),
            vm((8, width), F32),
            vm((2 * chan, width), BF16),
            vm((3, width, own_cols), BF16),
            vm((2, own_cols, half), BF16),
            vm((chan, width), BF16),
            vm((half, 2 * chan), BF16),
            vm((8, 2 * chan), F32),
            vm((txt, own_cols), BF16),
            vm((txt, own_cols), BF16),
            vm((own_cols, txt), BF16),
            vm((rows, 2 * chan), BF16),
            vm((rows, width), F32),
            vm((rows, width), BF16),
            vm((rows, own_cols), F32),
            vm((rows, own_cols), F32),
            vm((rows, own_cols), BF16),
            vm((rows, own_cols), BF16),
            vm((rows, own_cols), BF16),
            vm((heads, rows, rows + txt), BF16),
            vm((heads, rows, HD), F32),
            vm((rows, own_cols), BF16),
            vm((rows, own_cols), BF16),
            vm((rows, half), F32),
            vm((rows, half), F32),
            vm((rows, half), BF16),
            vm((3, tok, 2 * chan), F32),
            vm((3, tok, 2 * chan), F32),
            vm((3, tok, 2 * chan), F32),
            vm((ITERS, pack, 2 * chan), BF16),
            vm((ITERS, steps, pack, 2 * chan), BF16),
            dma((24,)),
            pltpu.SemaphoreType.REGULAR,
            dma((2,)),
            dma((2, pairs, 2)),
            dma((2,)),
            dma((ITERS,)),
            dma((ITERS, steps)),
        ],
        compiler_params=pltpu.CompilerParams(
            collective_id=0, has_side_effects=True, vmem_limit_bytes=55193 * 1024
        ),
        cost_estimate=pl.CostEstimate(
            flops=5 * 10**9, bytes_accessed=25 * 10**6, transcendentals=10**6
        ),
        name="picard",
    )(
        step_size,
        step_ids,
        noise,
        jnp.transpose(mod_table, (1, 0, 2)),
        w_in,
        jnp.transpose(w_qkv, (1, 0, 2)),
        w_out,
        jnp.transpose(w_final, (1, 0)),
        text_keys,
        text_values,
    )
    return out[None]


def solution(mesh):
    placed = (
        P(None, "seq", None),
        P("tm"),
        P("tm"),
        P(),
        P(),
        P(None, None, "seq"),
        P(),
        P(),
        P(None, "seq"),
        P(None, "seq"),
    )
    return jax.shard_map(
        per_device, mesh=mesh, in_specs=placed, out_specs=P("tm", "seq", None), check_vma=False
    )
```
